128 devices in a mesh: dp: 8 (over y, z_lo), tensor: 16 (over x, z_hi, core).
Axes of the slice: x: 4, y: 4, z: 4 (z_hi: 2, z_lo: 2; z = z_hi * 2 + z_lo), core: 2. Of those that a mesh axis runs over, the one named last changes fastest.
Arguments:
- attn_out: bfloat16 [8192, 2048], P('tensor', 'dp'), may hold values from -6 to 6
- o_proj: bfloat16 [4096, 8192], P(None, 'tensor'), may hold values from -0.0625 to 0.0625
- high_resid: bfloat16 [4096, 2048], P('tensor', 'dp'), may hold values from -6 to 6
- low_hidden: bfloat16 [4096, 2048], P('tensor', 'dp'), may hold values from -6 to 6
- mid_hidden: bfloat16 [4096, 2048], P('tensor', 'dp'), may hold values from -6 to 6
- route_list: int32 [2048], P('dp'), may hold values from 0 to 7, as said below
- fc_weight: bfloat16 [8, 4096, 3, 4096], P('dp', None, None, 'tensor'), may hold values from -0.0546875 to 0.0546875
- norm_gain: float32 [8, 4096], P('dp', 'tensor'), may hold values from 0.25 to 1.75
- cotangent: bfloat16 [4096, 2048], P('tensor', 'dp'), may hold values from -0.29882812 to 0.29882812
Outputs:
- draft_hidden: bfloat16 [4096, 2048], P('tensor', 'dp')
- fc_grad: float32 [8, 4096, 3, 4096], P('dp', None, None, 'tensor')
- gain_grad: float32 [8, 4096], P('dp', 'tensor')
The draws below stay inside these ranges and needn't reach their ends.
Inputs may be any that keep to these rules, and one draw needn't show every extreme that they name: `route_list`: in each replica's block of 256 tokens every trainer is named at most 128 times, and in every draw one trainer is named exactly 128 times in every block.
All inputs are finite; a program needn't handle non-finite values.
Results may differ from the reference program's by a relative error of at most 0.004.
Values may be sent and summed in bfloat16 or wider, within the bound.
No kernel may reach another device: no remote copies, remote signals or barrier semaphores. Data moves between devices by JAX's collectives and lax.ppermute only.
A program may use at most 128 MiB of HBM per device.

```python
import jax
import jax.numpy as jnp
from jax import lax

D = 8192
HW = 4096
DOUT = 4096
TOK_DEV = 256
CAP = 128
TOKENS = 2048
N_DP = 8


def draw_route_list(key, part):
    key = jax.random.fold_in(key, 11)
    key_busy, key_jitter, key_order = jax.random.split(key, 3)
    busiest = jax.random.randint(key_busy, (), 0, N_DP)
    position = jnp.arange(TOK_DEV, dtype=jnp.int32)
    limit = TOK_DEV // 2
    jitter = jax.random.randint(key_jitter, (N_DP, TOK_DEV), 0, 2)
    others = (position[None, :] + jitter) % (N_DP - 1)
    others = others + (others >= busiest).astype(jnp.int32)
    base = jnp.where(position[None, :] < limit, busiest, others)
    orders = jax.vmap(lambda one: jax.random.permutation(one, TOK_DEV))(jax.random.split(key_order, N_DP))
    routed = jnp.take_along_axis(base, orders, axis=1)
    return routed.reshape(-1).astype(jnp.int32)


def block_levels(own_key, extent, cuts, low, top_value):
    loudness = 1.0
    for axis_at, parts in cuts:
        draws = jax.random.uniform(jax.random.fold_in(jax.random.fold_in(own_key, 6), axis_at), (parts,), jnp.float32, low / len(cuts), top_value / len(cuts))
        loudness = loudness * jnp.repeat(jnp.exp(draws), extent[axis_at] // parts).reshape((-1,) + (1,) * (len(extent) - 1 - axis_at))
    return loudness


def bell_draw(own_key, dims, deviation, most, shards=(), held_as=jnp.bfloat16):
    result = jax.random.normal(own_key, dims, jnp.float32) * deviation
    if len(shards) > 0:
        result = block_levels(own_key, dims, shards, -0.22, 0.18) * result
    return jnp.clip(result, min=-most, max=most).astype(held_as)


def setup_inputs(seed: int = 0) -> dict:
    keys = jax.random.split(jax.random.key(seed), 10)
    attn_out = bell_draw(keys[0], (D, TOKENS), 1.0, 6.0, ((0, 16), (1, 8)))
    o_proj = bell_draw(keys[1], (HW, D), D ** -0.5, 0.0625, ((1, 16),))
    high_resid = bell_draw(keys[2], (HW, TOKENS), 1.0, 6.0, ((0, 16), (1, 8)))
    low_hidden = bell_draw(keys[3], (HW, TOKENS), 1.0, 6.0, ((0, 16), (1, 8)))
    mid_hidden = bell_draw(keys[4], (HW, TOKENS), 1.0, 6.0, ((0, 16), (1, 8)))
    route_list = draw_route_list(jax.random.fold_in(keys[9], 71), 0)
    fc_weight = bell_draw(keys[6], (N_DP, DOUT, 3, HW), (3 * HW) ** -0.5, 0.0546875, ((0, 8), (3, 16)))
    norm_gain = jnp.clip(1.0 + 0.15 * jax.random.normal(keys[7], (N_DP, DOUT), jnp.float32), 0.25, 1.75)
    cotangent = bell_draw(keys[8], (DOUT, TOKENS), 0.05, 0.29882812, ((0, 16), (1, 8)))
    return {"attn_out": attn_out, "o_proj": o_proj, "high_resid": high_resid, "low_hidden": low_hidden, "mid_hidden": mid_hidden, "route_list": route_list, "fc_weight": fc_weight, "norm_gain": norm_gain, "cotangent": cotangent}


epsilon = 1e-05

def reference(attn_out, o_proj, high_resid, low_hidden, mid_hidden, route_list, fc_weight, norm_gain, cotangent):
    high_term = jnp.dot(o_proj, attn_out, preferred_element_type=jnp.float32)
    high_hidden = (high_resid.astype(jnp.float32) + high_term).astype(jnp.bfloat16)
    stacked = jnp.concatenate([low_hidden, mid_hidden, high_hidden], axis=0)
    width = stacked.shape[0]
    slots = N_DP * CAP
    draft_hidden = jnp.zeros((DOUT, TOKENS), jnp.bfloat16)
    gain_rows = []
    grad_rows = []
    for trainer in range(N_DP):
        order = jnp.argsort((route_list != trainer).astype(jnp.int32), stable=True)[:slots].astype(jnp.int32)
        live = route_list[order] == trainer
        columns = jnp.where(live[None, :], stacked[:, order], jnp.zeros((), jnp.bfloat16))
        weight = fc_weight[trainer].reshape(DOUT, width)
        draft_pre = jnp.dot(weight, columns, preferred_element_type=jnp.float32)
        root_mean = jnp.sqrt(lax.optimization_barrier(jnp.sum(draft_pre * draft_pre, axis=0)) / DOUT + epsilon)
        normed = draft_pre / root_mean
        gain = norm_gain[trainer][:, None]
        outputs = (gain * normed).astype(jnp.bfloat16)
        draft_hidden = draft_hidden.at[:, order].add(jnp.where(live[None, :], outputs, jnp.zeros((), jnp.bfloat16)))
        upstream_raw = jnp.where(live[None, :], cotangent[:, order].astype(jnp.float32), jnp.float32(0.0))
        gain_rows.append(lax.optimization_barrier(jnp.sum(upstream_raw * normed, axis=1)))
        upstream = gain * upstream_raw
        slope = lax.optimization_barrier(jnp.sum(upstream * normed, axis=0))
        pre_grad = ((upstream - normed * slope / DOUT) / root_mean).astype(jnp.bfloat16)
        weight_grad = jnp.dot(pre_grad, columns.T, preferred_element_type=jnp.float32)
        grad_rows.append(weight_grad.reshape(DOUT, 3, HW))
    fc_grad = jnp.stack(grad_rows, axis=0)
    gain_grad = jnp.stack(gain_rows, axis=0)
    return (draft_hidden, fc_grad, gain_grad)
```

```python
import functools

import jax
import jax.numpy as jnp
from jax import lax
from jax.experimental import pallas as pl
from jax.experimental.pallas import tpu as pltpu
from jax.sharding import PartitionSpec as P

NX, NZ, NC = 4, 2, 2
NT = NX * NZ * NC
DOUT = 4096
HALF = DOUT // 2
EPS = 1e-05
F32, BF16 = jnp.float32, jnp.bfloat16
VMEM = 48 * 1024 * 1024


def shift(dx, dz, dc):
    pairs = []
    for x in range(NX):
        for z in range(NZ):
            for c in range(NC):
                pairs.append((x * 4 + z * 2 + c, (x + dx) % NX * 4 + (z ^ dz) * 2 + (c ^ dc)))
    return pairs


def send(v, dx=0, dz=0, dc=0):
    return lax.ppermute(v, "tensor", shift(dx, dz, dc))


def params():
    return pltpu.CompilerParams(vmem_limit_bytes=VMEM)


def nt(a, b):
    return lax.dot_general(a, b, (((1,), (1,)), ((), ())), preferred_element_type=F32)


def tn(a, b):
    return lax.dot_general(a, b, (((0,), (0,)), ((), ())), preferred_element_type=F32)


def oproj_kernel(pos, o_ref, a_ref, own_ref, oth_ref):
    z, c = pos[1], pos[2]
    for dz in range(NZ):
        for dc, out in ((0, own_ref), (1, oth_ref)):
            block = (z ^ dz) * 2 + (c ^ dc)
            rows = o_ref[pl.ds(pl.multiple_of(block * 256, 256), 256), :]
            out[0, dz] = jnp.dot(rows, a_ref[...], preferred_element_type=F32).astype(out.dtype)


def oproj_partial(pos, o_proj, attn):
    k, n = attn.shape
    part = lambda i, p: (i, 0, 0, 0)
    return pl.pallas_call(
        oproj_kernel,
        grid_spec=pltpu.PrefetchScalarGridSpec(
            num_scalar_prefetch=1,
            grid=(NX,),
            in_specs=[
                pl.BlockSpec((1024, k), lambda i, p: ((p[0] + i) % NX, 0)),
                pl.BlockSpec((k, n), lambda i, p: (0, 0)),
            ],
            out_specs=[pl.BlockSpec((1, NZ, 256, n), part)] * 2,
        ),
        out_shape=[jax.ShapeDtypeStruct((NX, NZ, 256, n), F32)] * 2,
        compiler_params=params(),
        name="oproj_partial",
    )(pos, o_proj, attn)


def reorder_kernel(pos, v_ref, own_ref, oth_ref):
    x, z, c = pos[0], pos[1], pos[2]
    for dx in range(NX):
        for dz in range(NZ):
            for dc, out in ((0, own_ref), (1, oth_ref)):
                t = ((x + dx) % NX) * 4 + (z ^ dz) * 2 + (c ^ dc)
                out[(dx * NZ + dz) * 64 : (dx * NZ + dz + 1) * 64, :] = v_ref[t]


def reorder(pos, v):
    f = v.shape[-1]
    whole = pl.BlockSpec(memory_space=pltpu.VMEM)
    return pl.pallas_call(
        reorder_kernel,
        in_specs=[pl.BlockSpec(memory_space=pltpu.SMEM), whole],
        out_specs=[whole] * 2,
        out_shape=[jax.ShapeDtypeStruct((512, f), v.dtype)] * 2,
        compiler_params=params(),
        name="reorder",
    )(pos, v.reshape(NT, 64, f))


def join_kernel(which, xo_ref, xp_ref, ho_ref, hp_ref, w_ref, v_ref, *outs):
    acc = nt(ho_ref[...], w_ref[2]) + nt(hp_ref[...], v_ref[2])
    for s in range(2):
        cols = slice(s * 256, (s + 1) * 256)
        acc += nt(xo_ref[:, cols], w_ref[s]) + nt(xp_ref[:, cols], v_ref[s])
    if which == 0:
        for dx in range(NX):
            outs[dx][...] = acc[dx * 128 : (dx + 1) * 128].astype(outs[dx].dtype)
    else:
        for dx in range(NX):
            for dz in range(NZ):
                at = dx * 128 + dz * 64
                outs[dz][dx * 64 : (dx + 1) * 64, :] = acc[at : at + 64].astype(outs[dz].dtype)


def join(which, xo, xp, ho, hp, w, v):
    tile = 512
    steps = HALF // tile
    base = which * steps
    whole = lambda a: pl.BlockSpec(a.shape, lambda j: (0, 0))
    wspec = pl.BlockSpec((3, tile, 256), lambda j: (0, base + j, 0))
    if which == 0:
        shapes = [(128, F32)] + [(128, BF16)] * 3
    else:
        shapes = [(256, F32), (256, BF16)]
    return pl.pallas_call(
        functools.partial(join_kernel, which),
        grid=(steps,),
        in_specs=[whole(xo), whole(xp), whole(ho), whole(hp), wspec, wspec],
        out_specs=[pl.BlockSpec((n, tile), lambda j: (0, j)) for n, _ in shapes],
        out_shape=[jax.ShapeDtypeStruct((n, HALF), t) for n, t in shapes],
        compiler_params=params(),
        name="join",
    )(xo, xp, ho, hp, w, v)


def norm_kernel(
    ka, ra, kb, rb1, rb2, rb3, cot_ref, gain_ref, out_ref, pga_ref, pgb_ref, pre
):
    per = HALF // 256
    square = jnp.zeros((64, 1), F32)
    inner = jnp.zeros((64, 1), F32)
    for t in range(NT):
        cols = slice(t % per * 256, (t % per + 1) * 256)
        if t < per:
            d = ka[:, cols] + ra[:, cols].astype(F32)
        else:
            d = kb[:, cols] + rb1[:, cols].astype(F32)
            d += rb2[:, cols].astype(F32) + rb3[:, cols].astype(F32)
        pre[t] = d
        up = gain_ref[t : t + 1, :] * cot_ref[t].astype(F32)
        square += jnp.sum(d * d, axis=1, keepdims=True)
        inner += jnp.sum(up * d, axis=1, keepdims=True)
    inv = 1.0 / jnp.sqrt(square / DOUT + EPS)
    slope = inner * inv
    for t in range(NT):
        cols = slice(t % per * 256, (t % per + 1) * 256)
        raw = cot_ref[t].astype(F32)
        gain = gain_ref[t : t + 1, :]
        normed = pre[t] * inv
        grad = ((gain * raw - normed * (slope / DOUT)) * inv).astype(BF16)
        if t < per:
            pga_ref[:, cols] = grad
        else:
            pgb_ref[:, cols] = grad
        total = jnp.sum(raw * normed, axis=0, keepdims=True)
        hi = total.astype(BF16)
        lo = (total - hi.astype(F32)).astype(BF16)
        row = lax.broadcasted_iota(jnp.int32, (16, 256), 0)
        extra = jnp.where(row == 0, hi.astype(F32), jnp.where(row == 1, lo.astype(F32), 0.0))
        out_ref[t, :64, :] = (gain * normed).astype(BF16)
        out_ref[t, 64:, :] = extra.astype(BF16)


def norm(ka, ra, kb, rb, cot, gain):
    whole = pl.BlockSpec(memory_space=pltpu.VMEM)
    return pl.pallas_call(
        norm_kernel,
        in_specs=[whole] * 8,
        out_specs=[whole] * 3,
        out_shape=[
            jax.ShapeDtypeStruct((NT, 80, 256), BF16),
            jax.ShapeDtypeStruct((64, HALF), BF16),
            jax.ShapeDtypeStruct((64, HALF), BF16),
        ],
        scratch_shapes=[pltpu.VMEM((NT, 64, 256), F32)],
        compiler_params=params(),
        name="norm",
    )(ka, ra, kb, *rb, cot, gain)


def grad_kernel(go_ref, gp_ref, xo_ref, xp_ref, ho_ref, hp_ref, *rest):
    out = rest[-1]
    go, gp = go_ref[...], gp_ref[...]
    for s in range(3):
        if s < 2:
            cols = slice(s * 256, (s + 1) * 256)
            a, b = xo_ref[:, cols], xp_ref[:, cols]
        else:
            a, b = ho_ref[...], hp_ref[...]
        out[s] = tn(go, a) + tn(gp, b)


def grad(which, go, gp, xo, xp, ho, hp, into=None):
    tile = 512
    steps = HALF // tile
    base = which * steps
    whole = lambda a: pl.BlockSpec(a.shape, lambda j: (0, 0))
    gspec = pl.BlockSpec((512, tile), lambda j: (0, j))
    specs = [gspec, gspec, whole(xo), whole(xp), whole(ho), whole(hp)]
    args = [go, gp, xo, xp, ho, hp]
    if into is not None:
        specs.append(pl.BlockSpec(memory_space=pl.ANY))
        args.append(into)
    return pl.pallas_call(
        grad_kernel,
        grid=(steps,),
        in_specs=specs,
        out_specs=pl.BlockSpec((3, tile, 256), lambda j: (0, base + j, 0)),
        out_shape=jax.ShapeDtypeStruct((3, DOUT, 256), F32),
        input_output_aliases={} if into is None else {6: 0},
        compiler_params=params(),
        name="grad",
    )(*args)


def local(
    attn_out,
    o_proj,
    high_resid,
    low_hidden,
    mid_hidden,
    route_list,
    fc_weight,
    norm_gain,
    cotangent,
):
    trainers = lax.axis_size("dp")
    toks = route_list.shape[0]
    cap = toks // 2
    slots = trainers * cap
    t = lax.axis_index("tensor")
    pos = jnp.stack([t // 4, t // 2 % 2, t % 2]).astype(jnp.int32)

    w = jnp.transpose(fc_weight[0], (1, 0, 2))
    w_other = send(w, dc=1)

    here = jnp.arange(toks, dtype=jnp.int32)
    same = (route_list[:, None] == route_list[None, :]) & (here[None, :] < here[:, None])
    slot = route_list * cap + jnp.sum(same.astype(jnp.int32), axis=1)
    pick = (slot[:, None] == jnp.arange(slots, dtype=jnp.int32)[None, :]).astype(BF16)

    def packed(v):
        rows = lax.dot_general(pick, v, (((0,), (1,)), ((), ())), preferred_element_type=BF16)
        return lax.all_to_all(rows.reshape(trainers, cap, -1), "dp", 0, 0)

    own, oth = oproj_partial(pos, o_proj, attn_out)
    own = own + send(oth, dc=1)
    narrow = own.astype(BF16)
    high = own[0, 0]
    for dx in range(NX):
        for dz in range(NZ):
            if dx or dz:
                high = high + send(narrow[dx, dz], dx, dz).astype(F32)
    high_hidden = (high_resid.astype(F32) + high).astype(BF16)

    early = packed(jnp.concatenate([low_hidden, mid_hidden, cotangent], axis=0))
    early = early.reshape(slots, -1)
    xo, xs = reorder(pos, early[:, :512])
    xp = send(xs, dc=1)
    cot = lax.all_to_all(early[:, 512:].reshape(NT, 64, 256), "tensor", 0, 0)
    gain = lax.all_gather(norm_gain[0], "tensor", axis=0)

    ho, hs = reorder(pos, packed(high_hidden).reshape(slots, -1))
    hp = send(hs, dc=1)

    a = join(0, xo, xp, ho, hp, w, w_other)
    ax = a[0]
    for dx in range(1, NX):
        ax = ax + send(a[dx], dx).astype(F32)
    b = join(1, xo, xp, ho, hp, w, w_other)
    bz = b[0] + send(b[1], dz=1).astype(F32)
    az = send(ax[64:].astype(BF16), dz=1)
    bx = [send(bz[dx * 64 : (dx + 1) * 64].astype(BF16), dx) for dx in range(1, NX)]

    outputs, ga, gb = norm(ax[:64], az, bz[:64], bx, cot, gain)

    def spread_z_first(v):
        far = send(v, dz=1)
        pieces = [v, far]
        for dx in range(1, NX):
            pieces += [send(v, -dx), send(far, -dx)]
        return jnp.concatenate(pieces, axis=0)

    def spread_x_first(v):
        pieces = []
        for dx in range(NX):
            near = send(v, -dx) if dx else v
            pieces += [near, send(near, dz=1)]
        return jnp.concatenate(pieces, axis=0)

    ga = spread_z_first(ga)
    gap = send(ga, dc=1)
    gb = spread_x_first(gb)
    gbp = send(gb, dc=1)
    fc = grad(0, ga, gap, xo, xs, ho, hs)
    fc = grad(1, gb, gbp, xo, xs, ho, hs, fc)
    fc_grad = jnp.transpose(fc, (1, 0, 2))[None]

    returned = lax.all_to_all(outputs, "tensor", 0, 0)
    gain_grad = jnp.sum(returned[:, 64:66].astype(F32), axis=(0, 1))[None, :]
    back = lax.all_to_all(returned[:, :64].reshape(trainers, cap, 256), "dp", 0, 0)
    draft_hidden = lax.dot_general(
        back.reshape(slots, 256), pick, (((0,), (1,)), ((), ())), preferred_element_type=BF16
    )
    return (draft_hidden, fc_grad, gain_grad)


def solution(mesh):
    return jax.shard_map(
        local,
        mesh=mesh,
        in_specs=(
            P("tensor", "dp"),
            P(None, "tensor"),
            P("tensor", "dp"),
            P("tensor", "dp"),
            P("tensor", "dp"),
            P("dp"),
            P("dp", None, None, "tensor"),
            P("dp", "tensor"),
            P("tensor", "dp"),
        ),
        out_specs=(P("tensor", "dp"), P("dp", None, None, "tensor"), P("dp", "tensor")),
        check_vma=False,
    )
```

```python
import functools

import jax
import jax.numpy as jnp
from jax import lax
from jax.experimental import pallas as pl
from jax.experimental.pallas import tpu as pltpu
from jax.sharding import PartitionSpec as P

NX, NZ, NC = 4, 2, 2
NT = NX * NZ * NC
DOUT = 4096
HALF = DOUT // 2
X_FIRST = 2048
EPS = 1e-05
F32, BF16 = jnp.float32, jnp.bfloat16
VMEM = 48 * 1024 * 1024
BIG = 40 * 1024 * 1024


def shift(dx, dz, dc):
    pairs = []
    for x in range(NX):
        for z in range(NZ):
            for c in range(NC):
                pairs.append((x * 4 + z * 2 + c, (x + dx) % NX * 4 + (z ^ dz) * 2 + (c ^ dc)))
    return pairs


def send(v, dx=0, dz=0, dc=0):
    return lax.ppermute(v, "tensor", shift(dx, dz, dc))


def params(limit=VMEM):
    return pltpu.CompilerParams(vmem_limit_bytes=limit)


def cost(macs, nbytes):
    return pl.CostEstimate(flops=2 * macs, bytes_accessed=nbytes, transcendentals=0)


def nt(a, b):
    return lax.dot_general(a, b, (((1,), (1,)), ((), ())), preferred_element_type=F32)


def tn(a, b):
    return lax.dot_general(a, b, (((0,), (0,)), ((), ())), preferred_element_type=F32)


def oproj_kernel(pos, o_ref, a_ref, own_ref, oth_ref):
    z, c = pos[1], pos[2]
    for dz in range(NZ):
        for dc, out in ((0, own_ref), (1, oth_ref)):
            block = (z ^ dz) * 2 + (c ^ dc)
            rows = o_ref[pl.ds(pl.multiple_of(block * 256, 256), 256), :]
            out[0, dz] = jnp.dot(rows, a_ref[...], preferred_element_type=F32)


def oproj_partial(pos, o_proj, attn):
    k, n = attn.shape
    return pl.pallas_call(
        oproj_kernel,
        grid_spec=pltpu.PrefetchScalarGridSpec(
            num_scalar_prefetch=1,
            grid=(NX,),
            in_specs=[
                pl.BlockSpec((1024, k), lambda i, p: ((p[0] + i) % NX, 0)),
                pl.BlockSpec((k, n), lambda i, p: (0, 0)),
            ],
            out_specs=[pl.BlockSpec((1, NZ, 256, n), lambda i, p: (i, 0, 0, 0))] * 2,
        ),
        out_shape=[jax.ShapeDtypeStruct((NX, NZ, 256, n), F32)] * 2,
        compiler_params=params(),
        cost_estimate=cost(DOUT * k * n, 9 << 20),
        name="oproj_partial",
    )(pos, o_proj, attn)


def join_kernel(which, xo_ref, xp_ref, ho_ref, hp_ref, w_ref, v_ref, *outs):
    acc = nt(ho_ref[...], w_ref[2]) + nt(hp_ref[...], v_ref[2])
    for s in range(2):
        cols = slice(s * 256, (s + 1) * 256)
        acc += nt(xo_ref[:, cols], w_ref[s]) + nt(xp_ref[:, cols], v_ref[s])
    if which == 0:
        for dx in range(NX):
            outs[dx][...] = acc[dx * 128 : (dx + 1) * 128].astype(outs[dx].dtype)
    else:
        for dx in range(NX):
            for dz in range(NZ):
                at = dx * 128 + dz * 64
                outs[dz][dx * 64 : (dx + 1) * 64, :] = acc[at : at + 64].astype(outs[dz].dtype)


def join(which, xo, xp, ho, hp, w, v):
    tile = 512
    width = X_FIRST if which == 0 else DOUT - X_FIRST
    base = X_FIRST // tile * which
    whole = lambda a: pl.BlockSpec(a.shape, lambda j: (0, 0))
    wspec = pl.BlockSpec((3, tile, 256), lambda j: (0, base + j, 0))
    if which == 0:
        shapes = [(128, F32)] + [(128, BF16)] * 3
    else:
        shapes = [(256, F32), (256, BF16)]
    return pl.pallas_call(
        functools.partial(join_kernel, which),
        grid=(width // tile,),
        in_specs=[whole(xo), whole(xp), whole(ho), whole(hp), wspec, wspec],
        out_specs=[pl.BlockSpec((n, tile), lambda j: (0, j)) for n, _ in shapes],
        out_shape=[jax.ShapeDtypeStruct((n, width), t) for n, t in shapes],
        compiler_params=params(),
        cost_estimate=cost(512 * 1536 * width, width * 4608),
        name="join",
    )(xo, xp, ho, hp, w, v)


def norm_kernel(
    ka, ra, kb, rb1, rb2, rb3, cot_ref, out_ref, pga_ref, pgb_ref, gg_ref, pre
):
    first, half = X_FIRST // 256, HALF // 256

    def gain_of(t):
        parts = cot_ref[t, 64:, :].astype(F32)
        return (parts[0:1] + parts[1:2]) + parts[2:3]

    square = jnp.zeros((64, 1), F32)
    inner = jnp.zeros((64, 1), F32)
    for t in range(NT):
        at = t if t < first else t - first
        cols = slice(at * 256, (at + 1) * 256)
        if t < first:
            d = ka[:, cols] + ra[:, cols].astype(F32)
        else:
            d = kb[:, cols] + rb1[:, cols].astype(F32)
            d += rb2[:, cols].astype(F32) + rb3[:, cols].astype(F32)
        pre[t] = d
        up = gain_of(t) * cot_ref[t, :64, :].astype(F32)
        square += jnp.sum(d * d, axis=1, keepdims=True)
        inner += jnp.sum(up * d, axis=1, keepdims=True)
    inv = 1.0 / jnp.sqrt(square / DOUT + EPS)
    slope = inner * inv
    row = lax.broadcasted_iota(jnp.int32, (16, 256), 0)
    for t in range(NT):
        cols = slice(t % half * 256, (t % half + 1) * 256)
        raw = cot_ref[t, :64, :].astype(F32)
        gain = gain_of(t)
        normed = pre[t] * inv
        grad = ((gain * raw - normed * (slope / DOUT)) * inv).astype(BF16)
        if t < half:
            pga_ref[:, cols] = grad
        else:
            pgb_ref[:, cols] = grad
        total = jnp.sum(raw * normed, axis=0, keepdims=True)
        hi = total.astype(BF16).astype(F32)
        extra = jnp.where(row == 0, hi, jnp.where(row == 1, total - hi, 0.0))
        gg_ref[t] = extra.astype(BF16)
        out_ref[t] = (gain * normed).astype(BF16)


def norm(ka, ra, kb, rb, cot):
    whole = pl.BlockSpec(memory_space=pltpu.VMEM)
    return pl.pallas_call(
        norm_kernel,
        in_specs=[whole] * 7,
        out_specs=[whole] * 4,
        out_shape=[
            jax.ShapeDtypeStruct((NT, 64, 256), BF16),
            jax.ShapeDtypeStruct((64, HALF), BF16),
            jax.ShapeDtypeStruct((64, HALF), BF16),
            jax.ShapeDtypeStruct((NT, 16, 256), BF16),
        ],
        scratch_shapes=[pltpu.VMEM((NT, 64, 256), F32)],
        compiler_params=params(),
        cost_estimate=cost(0, 6 << 20),
        name="norm",
    )(ka, ra, kb, *rb, cot)


def grad_kernel(ng, *refs):
    out = refs[-1]
    g = jnp.concatenate([g[...] for g in refs[:ng]], axis=0)
    both = tn(g, refs[ng][...])
    for s in range(3):
        out[s] = both[:, s * 256 : (s + 1) * 256]


def grad(which, gs, x, into=None):
    tile = 512
    steps = HALF // tile
    base = which * steps
    specs = [pl.BlockSpec((g.shape[0], tile), lambda j: (0, j)) for g in gs]
    specs.append(pl.BlockSpec(x.shape, lambda j: (0, 0)))
    args = list(gs) + [x]
    if into is not None:
        specs.append(pl.BlockSpec(memory_space=pl.ANY))
        args.append(into)
    return pl.pallas_call(
        functools.partial(grad_kernel, len(gs)),
        grid=(steps,),
        in_specs=specs,
        out_specs=pl.BlockSpec((3, tile, 256), lambda j: (0, base + j, 0)),
        out_shape=jax.ShapeDtypeStruct((3, DOUT, 256), F32),
        input_output_aliases={} if into is None else {len(args) - 1: 0},
        compiler_params=params(BIG),
        cost_estimate=cost(1024 * 768 * HALF, 12 << 20),
        name="grad",
    )(*args)


def local(
    attn_out,
    o_proj,
    high_resid,
    low_hidden,
    mid_hidden,
    route_list,
    fc_weight,
    norm_gain,
    cotangent,
):
    trainers = lax.axis_size("dp")
    toks = route_list.shape[0]
    cap = toks // 2
    slots = trainers * cap
    t = lax.axis_index("tensor")
    x, z, c = t // 4, t // 2 % 2, t % 2
    pos = jnp.stack([x, z, c]).astype(jnp.int32)

    here = jnp.arange(toks, dtype=jnp.int32)
    same = (route_list[:, None] == route_list[None, :]) & (here[None, :] < here[:, None])
    within = jnp.sum(same.astype(jnp.int32), axis=1)

    def onehot(slot, n):
        return (slot[:, None] == jnp.arange(n, dtype=jnp.int32)[None, :]).astype(BF16)

    pick = onehot(route_list * cap + within, slots)
    back_pick = onehot(within // 8 * 80 + route_list * 8 + within % 8, NT * 80)

    at = jnp.arange(slots, dtype=jnp.int32)
    inner = at // 8 % 8 * cap + at % 8
    block = at // 64

    def device(dc, dx, dz):
        return (x + dx) % 4 * 4 + (z ^ dz) * 2 + (c ^ dc)

    straight = onehot(inner + block * 8, slots)
    from_a = device(block // 8, block // 2 % 4, block % 2) * 8
    order_a = onehot(inner + from_a, slots)
    y, zl = lax.axis_index("dp") // 2, lax.axis_index("dp") % 2
    replica = at // 8 % 8
    apart = (y - replica // 2 + 4) % 4 * 2 + (replica % 2 ^ zl)
    near_order = onehot(apart * cap + at % 8 + from_a, slots)
    towards = (route_list % 2 ^ zl) * 4 + (route_list // 2 - y + 4) % 4
    near_pick = onehot(towards * cap + within, slots)
    order_b = onehot((block // 8 * 8 + block % 4 * 2 + block // 4 % 2) * 64 + at % 64, slots)

    def moved(order, v):
        return jnp.dot(order, v, preferred_element_type=BF16)

    def packed(pick, v):
        return lax.dot_general(pick, v, (((0,), (1,)), ((), ())), preferred_element_type=BF16)

    early = packed(pick, jnp.concatenate([low_hidden, mid_hidden, cotangent], axis=0))
    early = lax.all_to_all(early.reshape(trainers, cap, -1), "dp", 0, 0).reshape(slots, -1)

    own, oth = oproj_partial(pos, o_proj, attn_out)
    own = own + send(oth, dc=1)
    w = jnp.transpose(fc_weight[0], (1, 0, 2))
    w, own = lax.optimization_barrier((w, own))
    w_other = send(w, dc=1)
    narrow = own.astype(BF16)
    sums = own[0]
    for dx in range(1, NX):
        sums = sums + send(narrow[dx], dx).astype(F32)
    term = sums[0] + send(sums[1], dz=1)
    high_hidden = (high_resid.astype(F32) + term).astype(BF16)

    early, high_hidden = lax.optimization_barrier((early, high_hidden))

    gain = norm_gain[0]
    part0 = lax.reduce_precision(gain, 8, 7)
    part1 = lax.reduce_precision(gain - part0, 8, 7)
    part2 = gain - part0 - part1
    parts = jnp.pad(jnp.stack([part0, part1, part2]).astype(BF16), ((0, 13), (0, 0)))
    cot = jnp.concatenate(
        [
            moved(straight, early[:, 512:]).reshape(NT, 64, 256),
            jnp.broadcast_to(parts[None], (NT, 16, 256)),
        ],
        axis=1,
    )
    cot = lax.all_to_all(cot, "tensor", 0, 0)

    lowmid = early[:, :512]
    keep, other = [packed(near_pick[:, i * 512 : (i + 1) * 512], high_hidden) for i in range(2)]
    got = lax.ppermute(other, "dp", [(i, i ^ 1) for i in range(8)])
    pair = jnp.stack([keep.reshape(4, cap, -1), got.reshape(4, cap, -1)], axis=1)
    far = [
        lax.ppermute(pair[dy], "dp", [(i, (i + 2 * dy) % 8) for i in range(8)])
        for dy in range(1, 4)
    ]
    high_rows = jnp.concatenate([pair[0]] + far, axis=0).reshape(slots, -1)
    xo, xs = moved(order_a[:512], lowmid), moved(order_a[512:], lowmid)
    xp = send(xs, dc=1)
    ho, hs = moved(near_order[:512], high_rows), moved(near_order[512:], high_rows)
    hp = send(hs, dc=1)
    ho, hp, cot = lax.optimization_barrier((ho, hp, cot))

    b = join(1, xo, xp, ho, hp, w, w_other)
    bz = b[0] + send(b[1], dz=1).astype(F32)
    a = join(0, xo, xp, ho, hp, w, w_other)
    a, xs, hs = lax.optimization_barrier((a, xs, hs))
    got = [send(a[dx], dx) for dx in range(1, NX)]
    got, _ = lax.optimization_barrier((got, bz))
    ax = a[0] + got[0].astype(F32) + got[1].astype(F32) + got[2].astype(F32)
    az = send(ax[64:].astype(BF16), dz=1)
    bx = [send(bz[dx * 64 : (dx + 1) * 64].astype(BF16), dx) for dx in range(1, NX)]

    xa = jnp.concatenate(
        [jnp.concatenate([xo, xs], axis=0), jnp.concatenate([ho, hs], axis=0)], axis=1
    )
    xb = moved(order_b, xa)
    xa, xb, az = lax.optimization_barrier((xa, xb, az))

    outputs, ga, gb, gg = norm(ax[:64], az, bz[:64], bx, cot)

    far = send(ga, dz=1)
    near = [send(gb, -dx) for dx in range(1, NX)]
    outputs = outputs.reshape(NT, trainers, 8, 256).transpose(1, 0, 2, 3)
    outputs = lax.all_to_all(outputs, "dp", 0, 0)
    a0 = jnp.concatenate([ga, far], axis=0)
    near, _, outputs = lax.optimization_barrier((near, a0, outputs))
    b0 = jnp.concatenate([gb] + near, axis=0)
    a1 = [send(a0, -dx) for dx in range(1, NX)]
    b1 = send(b0, dz=1)
    a0p, b0p = send(a0, dc=1), send(b0, dc=1)
    outputs = outputs.transpose(1, 0, 2, 3).reshape(NT, 64, 256)
    outputs = jnp.concatenate([outputs, gg], axis=1)
    a1p, b1p = [send(v, dc=1) for v in a1], send(b1, dc=1)
    returned = lax.all_to_all(outputs, "tensor", 0, 0)
    fc = grad(0, [a0] + a1 + [a0p] + a1p, xa)
    fc = grad(1, (b0, b1, b0p, b1p), xb, fc)
    returned, fc = lax.optimization_barrier((returned, fc))
    gain_grad = jnp.sum(returned[:, 64:66].astype(F32), axis=(0, 1))[None, :]
    draft_hidden = lax.dot_general(
        returned.reshape(NT * 80, 256),
        back_pick,
        (((0,), (1,)), ((), ())),
        preferred_element_type=BF16,
    )
    fc_grad = jnp.transpose(fc, (1, 0, 2))[None]
    return (draft_hidden, fc_grad, gain_grad)


def solution(mesh):
    return jax.shard_map(
        local,
        mesh=mesh,
        in_specs=(
            P("tensor", "dp"),
            P(None, "tensor"),
            P("tensor", "dp"),
            P("tensor", "dp"),
            P("tensor", "dp"),
            P("dp"),
            P("dp", None, None, "tensor"),
            P("dp", "tensor"),
            P("tensor", "dp"),
        ),
        out_specs=(P("tensor", "dp"), P("dp", None, None, "tensor"), P("dp", "tensor")),
        check_vma=False,
    )
```

```python
import functools

import jax
import jax.numpy as jnp
from jax import lax
from jax.experimental import pallas as pl
from jax.experimental.pallas import tpu as pltpu
from jax.sharding import PartitionSpec as P

NX, NZ, NC = 4, 2, 2
NT = NX * NZ * NC
DOUT = 4096
HALF = DOUT // 2
X_FIRST = 2048
EPS = 1e-05
F32, BF16 = jnp.float32, jnp.bfloat16
VMEM = 48 * 1024 * 1024
BIG = 40 * 1024 * 1024


def shift(dx, dz, dc):
    pairs = []
    for x in range(NX):
        for z in range(NZ):
            for c in range(NC):
                pairs.append((x * 4 + z * 2 + c, (x + dx) % NX * 4 + (z ^ dz) * 2 + (c ^ dc)))
    return pairs


def send(v, dx=0, dz=0, dc=0):
    return lax.ppermute(v, "tensor", shift(dx, dz, dc))


def params(limit=VMEM):
    return pltpu.CompilerParams(vmem_limit_bytes=limit)


def cost(macs, nbytes):
    return pl.CostEstimate(flops=2 * macs, bytes_accessed=nbytes, transcendentals=0)


def nt(a, b):
    return lax.dot_general(a, b, (((1,), (1,)), ((), ())), preferred_element_type=F32)


def tn(a, b):
    return lax.dot_general(a, b, (((0,), (0,)), ((), ())), preferred_element_type=F32)


def oproj_kernel(pos, o_ref, a_ref, own_ref, oth_ref):
    z, c = pos[1], pos[2]
    for dz in range(NZ):
        for dc, out in ((0, own_ref), (1, oth_ref)):
            block = (z ^ dz) * 2 + (c ^ dc)
            rows = o_ref[pl.ds(pl.multiple_of(block * 256, 256), 256), :]
            out[0, dz] = jnp.dot(rows, a_ref[...], preferred_element_type=F32)


def oproj_partial(pos, o_proj, attn):
    k, n = attn.shape
    return pl.pallas_call(
        oproj_kernel,
        grid_spec=pltpu.PrefetchScalarGridSpec(
            num_scalar_prefetch=1,
            grid=(NX,),
            in_specs=[
                pl.BlockSpec((1024, k), lambda i, p: ((p[0] + i) % NX, 0)),
                pl.BlockSpec((k, n), lambda i, p: (0, 0)),
            ],
            out_specs=[pl.BlockSpec((1, NZ, 256, n), lambda i, p: (i, 0, 0, 0))] * 2,
        ),
        out_shape=[jax.ShapeDtypeStruct((NX, NZ, 256, n), F32)] * 2,
        compiler_params=params(),
        cost_estimate=cost(DOUT * k * n, 9 << 20),
        name="oproj_partial",
    )(pos, o_proj, attn)


def join_kernel(which, xo_ref, xp_ref, ho_ref, hp_ref, w_ref, v_ref, *outs):
    acc = nt(ho_ref[...], w_ref[2]) + nt(hp_ref[...], v_ref[2])
    for s in range(2):
        cols = slice(s * 256, (s + 1) * 256)
        acc += nt(xo_ref[:, cols], w_ref[s]) + nt(xp_ref[:, cols], v_ref[s])
    if which == 0:
        for dx in range(NX):
            outs[dx][...] = acc[dx * 128 : (dx + 1) * 128].astype(outs[dx].dtype)
    else:
        for dx in range(NX):
            for dz in range(NZ):
                at = dx * 128 + dz * 64
                outs[dz][dx * 64 : (dx + 1) * 64, :] = acc[at : at + 64].astype(outs[dz].dtype)


def join(which, xo, xp, ho, hp, w, v):
    tile = 512
    width = X_FIRST if which == 0 else DOUT - X_FIRST
    base = X_FIRST // tile * which
    whole = lambda a: pl.BlockSpec(a.shape, lambda j: (0, 0))
    wspec = pl.BlockSpec((3, tile, 256), lambda j: (0, base + j, 0))
    if which == 0:
        shapes = [(128, F32)] + [(128, BF16)] * 3
    else:
        shapes = [(256, F32), (256, BF16)]
    return pl.pallas_call(
        functools.partial(join_kernel, which),
        grid=(width // tile,),
        in_specs=[whole(xo), whole(xp), whole(ho), whole(hp), wspec, wspec],
        out_specs=[pl.BlockSpec((n, tile), lambda j: (0, j)) for n, _ in shapes],
        out_shape=[jax.ShapeDtypeStruct((n, width), t) for n, t in shapes],
        compiler_params=params(),
        cost_estimate=cost(512 * 1536 * width, width * 4608),
        name="join",
    )(xo, xp, ho, hp, w, v)


def norm_kernel(
    ka, ra, kb, rb1, rb2, rb3, cot_ref, out_ref, pga_ref, pgb_ref, gg_ref, pre
):
    first, half = X_FIRST // 256, HALF // 256

    def gain_of(t):
        parts = cot_ref[t, 64:, :].astype(F32)
        return (parts[0:1] + parts[1:2]) + parts[2:3]

    square = jnp.zeros((64, 1), F32)
    inner = jnp.zeros((64, 1), F32)
    for t in range(NT):
        at = t if t < first else t - first
        cols = slice(at * 256, (at + 1) * 256)
        if t < first:
            d = ka[:, cols] + ra[:, cols].astype(F32)
        else:
            d = kb[:, cols] + rb1[:, cols].astype(F32)
            d += rb2[:, cols].astype(F32) + rb3[:, cols].astype(F32)
        pre[t] = d
        up = gain_of(t) * cot_ref[t, :64, :].astype(F32)
        square += jnp.sum(d * d, axis=1, keepdims=True)
        inner += jnp.sum(up * d, axis=1, keepdims=True)
    inv = 1.0 / jnp.sqrt(square / DOUT + EPS)
    slope = inner * inv
    row = lax.broadcasted_iota(jnp.int32, (16, 256), 0)
    for t in range(NT):
        cols = slice(t % half * 256, (t % half + 1) * 256)
        raw = cot_ref[t, :64, :].astype(F32)
        gain = gain_of(t)
        normed = pre[t] * inv
        grad = ((gain * raw - normed * (slope / DOUT)) * inv).astype(BF16)
        if t < half:
            pga_ref[:, cols] = grad
        else:
            pgb_ref[:, cols] = grad
        total = jnp.sum(raw * normed, axis=0, keepdims=True)
        hi = total.astype(BF16).astype(F32)
        extra = jnp.where(row == 0, hi, jnp.where(row == 1, total - hi, 0.0))
        gg_ref[t] = extra.astype(BF16)
        out_ref[t] = (gain * normed).astype(BF16)


def norm(ka, ra, kb, rb, cot):
    whole = pl.BlockSpec(memory_space=pltpu.VMEM)
    return pl.pallas_call(
        norm_kernel,
        in_specs=[whole] * 7,
        out_specs=[whole] * 4,
        out_shape=[
            jax.ShapeDtypeStruct((NT, 64, 256), BF16),
            jax.ShapeDtypeStruct((64, HALF), BF16),
            jax.ShapeDtypeStruct((64, HALF), BF16),
            jax.ShapeDtypeStruct((NT, 16, 256), BF16),
        ],
        scratch_shapes=[pltpu.VMEM((NT, 64, 256), F32)],
        compiler_params=params(),
        cost_estimate=cost(0, 6 << 20),
        name="norm",
    )(ka, ra, kb, *rb, cot)


def grad_kernel(ng, *refs):
    out = refs[-1]
    g = jnp.concatenate([g[...] for g in refs[:ng]], axis=0)
    both = tn(g, refs[ng][...])
    for s in range(3):
        out[s] = both[:, s * 256 : (s + 1) * 256]


def grad(which, gs, x, into=None):
    tile = 512
    steps = HALF // tile
    base = which * steps
    specs = [pl.BlockSpec((g.shape[0], tile), lambda j: (0, j)) for g in gs]
    specs.append(pl.BlockSpec(x.shape, lambda j: (0, 0)))
    args = list(gs) + [x]
    if into is not None:
        specs.append(pl.BlockSpec(memory_space=pl.ANY))
        args.append(into)
    return pl.pallas_call(
        functools.partial(grad_kernel, len(gs)),
        grid=(steps,),
        in_specs=specs,
        out_specs=pl.BlockSpec((3, tile, 256), lambda j: (0, base + j, 0)),
        out_shape=jax.ShapeDtypeStruct((3, DOUT, 256), F32),
        input_output_aliases={} if into is None else {len(args) - 1: 0},
        compiler_params=params(BIG),
        cost_estimate=cost(1024 * 768 * HALF, 12 << 20),
        name="grad",
    )(*args)


def local(
    attn_out,
    o_proj,
    high_resid,
    low_hidden,
    mid_hidden,
    route_list,
    fc_weight,
    norm_gain,
    cotangent,
):
    trainers = lax.axis_size("dp")
    toks = route_list.shape[0]
    cap = toks // 2
    slots = trainers * cap
    t = lax.axis_index("tensor")
    x, z, c = t // 4, t // 2 % 2, t % 2
    pos = jnp.stack([x, z, c]).astype(jnp.int32)

    here = jnp.arange(toks, dtype=jnp.int32)
    same = (route_list[:, None] == route_list[None, :]) & (here[None, :] < here[:, None])
    within = jnp.sum(same.astype(jnp.int32), axis=1)

    def onehot(slot, n):
        return (slot[:, None] == jnp.arange(n, dtype=jnp.int32)[None, :]).astype(BF16)

    pick = onehot(route_list * cap + within, slots)
    back_pick = onehot(within // 8 * 80 + route_list * 8 + within % 8, NT * 80)

    def moved(order, v):
        return jnp.dot(order, v, preferred_element_type=BF16)

    def packed(pick, v):
        return lax.dot_general(pick, v, (((0,), (1,)), ((), ())), preferred_element_type=BF16)

    early = packed(pick, jnp.concatenate([low_hidden, mid_hidden, cotangent], axis=0))
    early = lax.all_to_all(early.reshape(trainers, cap, -1), "dp", 0, 0).reshape(slots, -1)

    own, oth = oproj_partial(pos, o_proj, attn_out)
    own = own + send(oth, dc=1)
    w = jnp.transpose(fc_weight[0], (1, 0, 2))
    w, own = lax.optimization_barrier((w, own))
    w_other = send(w, dc=1)
    narrow = own.astype(BF16)
    sums = own[0]
    for dx in range(1, NX):
        sums = sums + send(narrow[dx], dx).astype(F32)
    at = jnp.arange(slots, dtype=jnp.int32)
    at, sums = lax.optimization_barrier((at, sums))
    inner = at // 8 % 8 * cap + at % 8
    block = at // 64

    def device(dc, dx, dz):
        return (x + dx) % 4 * 4 + (z ^ dz) * 2 + (c ^ dc)

    straight = onehot(inner + block * 8, slots)
    from_a = device(block // 8, block // 2 % 4, block % 2) * 8
    order_a = onehot(inner + from_a, slots)
    y, zl = lax.axis_index("dp") // 2, lax.axis_index("dp") % 2
    replica = at // 8 % 8
    apart = (y - replica // 2 + 4) % 4 * 2 + (replica % 2 ^ zl)
    near_order = onehot(apart * cap + at % 8 + from_a, slots)
    towards = (route_list % 2 ^ zl) * 4 + (route_list // 2 - y + 4) % 4
    near_pick = onehot(towards * cap + within, slots)
    order_b = onehot((block // 8 * 8 + block % 4 * 2 + block // 4 % 2) * 64 + at % 64, slots)

    term = sums[0] + send(sums[1], dz=1)
    high_hidden = (high_resid.astype(F32) + term).astype(BF16)

    early, high_hidden = lax.optimization_barrier((early, high_hidden))

    gain = norm_gain[0]
    part0 = lax.reduce_precision(gain, 8, 7)
    part1 = lax.reduce_precision(gain - part0, 8, 7)
    part2 = gain - part0 - part1
    parts = jnp.pad(jnp.stack([part0, part1, part2]).astype(BF16), ((0, 13), (0, 0)))
    cot = jnp.concatenate(
        [
            moved(straight, early[:, 512:]).reshape(NT, 64, 256),
            jnp.broadcast_to(parts[None], (NT, 16, 256)),
        ],
        axis=1,
    )
    cot = lax.all_to_all(cot, "tensor", 0, 0)

    lowmid = early[:, :512]
    keep, other = [packed(near_pick[:, i * 512 : (i + 1) * 512], high_hidden) for i in range(2)]
    got = lax.ppermute(other, "dp", [(i, i ^ 1) for i in range(8)])
    pair = jnp.stack([keep.reshape(4, cap, -1), got.reshape(4, cap, -1)], axis=1)
    far = [
        lax.ppermute(pair[dy], "dp", [(i, (i + 2 * dy) % 8) for i in range(8)])
        for dy in range(1, 4)
    ]
    high_rows = jnp.concatenate([pair[0]] + far, axis=0).reshape(slots, -1)
    xo, xs = moved(order_a[:512], lowmid), moved(order_a[512:], lowmid)
    xp = send(xs, dc=1)
    ho, hs = moved(near_order[:512], high_rows), moved(near_order[512:], high_rows)
    hp = send(hs, dc=1)
    ho, hp, cot = lax.optimization_barrier((ho, hp, cot))

    b = join(1, xo, xp, ho, hp, w, w_other)
    bz = b[0] + send(b[1], dz=1).astype(F32)
    a = join(0, xo, xp, ho, hp, w, w_other)
    a, xs, hs = lax.optimization_barrier((a, xs, hs))
    got = [send(a[dx], dx) for dx in range(1, NX)]
    got, _ = lax.optimization_barrier((got, bz))
    ax = a[0] + got[0].astype(F32) + got[1].astype(F32) + got[2].astype(F32)
    az = send(ax[64:].astype(BF16), dz=1)
    bx = [send(bz[dx * 64 : (dx + 1) * 64].astype(BF16), dx) for dx in range(1, NX)]

    xa = jnp.concatenate(
        [jnp.concatenate([xo, xs], axis=0), jnp.concatenate([ho, hs], axis=0)], axis=1
    )
    xb = moved(order_b, xa)
    xa, xb, az = lax.optimization_barrier((xa, xb, az))

    outputs, ga, gb, gg = norm(ax[:64], az, bz[:64], bx, cot)

    far = send(ga, dz=1)
    near = [send(gb, -dx) for dx in range(1, NX)]
    outputs = outputs.reshape(NT, trainers, 8, 256).transpose(1, 0, 2, 3)
    outputs = lax.all_to_all(outputs, "dp", 0, 0)
    a0 = jnp.concatenate([ga, far], axis=0)
    near, _, outputs = lax.optimization_barrier((near, a0, outputs))
    b0 = jnp.concatenate([gb] + near, axis=0)
    a1 = [send(a0, -dx) for dx in range(1, NX)]
    b1 = send(b0, dz=1)
    a0p, b0p = send(a0, dc=1), send(b0, dc=1)
    outputs = outputs.transpose(1, 0, 2, 3).reshape(NT, 64, 256)
    outputs = jnp.concatenate([outputs, gg], axis=1)
    a1[0], outputs = lax.optimization_barrier((a1[0], outputs))
    a1p, b1p = [send(v, dc=1) for v in a1], send(b1, dc=1)
    returned = lax.all_to_all(outputs, "tensor", 0, 0)
    fc = grad(0, [a0] + a1 + [a0p] + a1p, xa)
    fc = grad(1, (b0, b1, b0p, b1p), xb, fc)
    returned, fc = lax.optimization_barrier((returned, fc))
    gain_grad = jnp.sum(returned[:, 64:66].astype(F32), axis=(0, 1))[None, :]
    draft_hidden = lax.dot_general(
        returned.reshape(NT * 80, 256),
        back_pick,
        (((0,), (1,)), ((), ())),
        preferred_element_type=BF16,
    )
    fc_grad = jnp.transpose(fc, (1, 0, 2))[None]
    return (draft_hidden, fc_grad, gain_grad)


def solution(mesh):
    return jax.shard_map(
        local,
        mesh=mesh,
        in_specs=(
            P("tensor", "dp"),
            P(None, "tensor"),
            P("tensor", "dp"),
            P("tensor", "dp"),
            P("tensor", "dp"),
            P("dp"),
            P("dp", None, None, "tensor"),
            P("dp", "tensor"),
            P("tensor", "dp"),
        ),
        out_specs=(P("tensor", "dp"), P("dp", None, None, "tensor"), P("dp", "tensor")),
        check_vma=False,
    )
```

```python
import functools

import jax
import jax.numpy as jnp
from jax import lax
from jax.experimental import pallas as pl
from jax.experimental.pallas import tpu as pltpu
from jax.sharding import PartitionSpec as P

NX, NZ, NC = 4, 2, 2
NT = NX * NZ * NC
DOUT = 4096
HALF = DOUT // 2
X_FIRST = 2048
EPS = 1e-05
F32, BF16 = jnp.float32, jnp.bfloat16
VMEM = 48 * 1024 * 1024
BIG = 40 * 1024 * 1024


def shift(dx, dz, dc):
    pairs = []
    for x in range(NX):
        for z in range(NZ):
            for c in range(NC):
                pairs.append((x * 4 + z * 2 + c, (x + dx) % NX * 4 + (z ^ dz) * 2 + (c ^ dc)))
    return pairs


def send(v, dx=0, dz=0, dc=0):
    return lax.ppermute(v, "tensor", shift(dx, dz, dc))


def params(limit=VMEM):
    return pltpu.CompilerParams(vmem_limit_bytes=limit)


def cost(macs, nbytes):
    return pl.CostEstimate(flops=2 * macs, bytes_accessed=nbytes, transcendentals=0)


def nt(a, b):
    return lax.dot_general(a, b, (((1,), (1,)), ((), ())), preferred_element_type=F32)


def tn(a, b):
    return lax.dot_general(a, b, (((0,), (0,)), ((), ())), preferred_element_type=F32)


def oproj_kernel(pos, o_ref, a_ref, own_ref, oth_ref):
    z, c = pos[1], pos[2]
    for dz in range(NZ):
        for dc, out in ((0, own_ref), (1, oth_ref)):
            block = (z ^ dz) * 2 + (c ^ dc)
            rows = o_ref[pl.ds(pl.multiple_of(block * 256, 256), 256), :]
            out[0, dz] = jnp.dot(rows, a_ref[...], preferred_element_type=F32)


def oproj_partial(pos, o_proj, attn):
    k, n = attn.shape
    return pl.pallas_call(
        oproj_kernel,
        grid_spec=pltpu.PrefetchScalarGridSpec(
            num_scalar_prefetch=1,
            grid=(NX,),
            in_specs=[
                pl.BlockSpec((1024, k), lambda i, p: ((p[0] + i) % NX, 0)),
                pl.BlockSpec((k, n), lambda i, p: (0, 0)),
            ],
            out_specs=[pl.BlockSpec((1, NZ, 256, n), lambda i, p: (i, 0, 0, 0))] * 2,
        ),
        out_shape=[jax.ShapeDtypeStruct((NX, NZ, 256, n), F32)] * 2,
        compiler_params=params(),
        cost_estimate=cost(DOUT * k * n, 9 << 20),
        name="oproj_partial",
    )(pos, o_proj, attn)


def join_kernel(which, xo_ref, xp_ref, ho_ref, hp_ref, w_ref, v_ref, *outs):
    acc = nt(ho_ref[...], w_ref[2]) + nt(hp_ref[...], v_ref[2])
    for s in range(2):
        cols = slice(s * 256, (s + 1) * 256)
        acc += nt(xo_ref[:, cols], w_ref[s]) + nt(xp_ref[:, cols], v_ref[s])
    if which == 0:
        for dx in range(NX):
            outs[dx][...] = acc[dx * 128 : (dx + 1) * 128].astype(outs[dx].dtype)
    else:
        for dx in range(NX):
            for dz in range(NZ):
                at = dx * 128 + dz * 64
                outs[dz][dx * 64 : (dx + 1) * 64, :] = acc[at : at + 64].astype(outs[dz].dtype)


def join(which, xo, xp, ho, hp, w, v):
    tile = 512
    width = X_FIRST if which == 0 else DOUT - X_FIRST
    base = X_FIRST // tile * which
    whole = lambda a: pl.BlockSpec(a.shape, lambda j: (0, 0))
    wspec = pl.BlockSpec((3, tile, 256), lambda j: (0, base + j, 0))
    if which == 0:
        shapes = [(128, F32)] + [(128, BF16)] * 3
    else:
        shapes = [(256, F32), (256, BF16)]
    return pl.pallas_call(
        functools.partial(join_kernel, which),
        grid=(width // tile,),
        in_specs=[whole(xo), whole(xp), whole(ho), whole(hp), wspec, wspec],
        out_specs=[pl.BlockSpec((n, tile), lambda j: (0, j)) for n, _ in shapes],
        out_shape=[jax.ShapeDtypeStruct((n, width), t) for n, t in shapes],
        compiler_params=params(),
        cost_estimate=cost(512 * 1536 * width, width * 4608),
        name="join",
    )(xo, xp, ho, hp, w, v)


def norm_kernel(
    ka, ra, kb, rb1, rb2, rb3, cot_ref, out_ref, pga_ref, pgb_ref, gg_ref, pre
):
    first, half = X_FIRST // 256, HALF // 256

    def gain_of(t):
        parts = cot_ref[t, 64:, :].astype(F32)
        return (parts[0:1] + parts[1:2]) + parts[2:3]

    square = jnp.zeros((64, 1), F32)
    inner = jnp.zeros((64, 1), F32)
    for t in range(NT):
        at = t if t < first else t - first
        cols = slice(at * 256, (at + 1) * 256)
        if t < first:
            d = ka[:, cols] + ra[:, cols].astype(F32)
        else:
            d = kb[:, cols] + rb1[:, cols].astype(F32)
            d += rb2[:, cols].astype(F32) + rb3[:, cols].astype(F32)
        pre[t] = d
        up = gain_of(t) * cot_ref[t, :64, :].astype(F32)
        square += jnp.sum(d * d, axis=1, keepdims=True)
        inner += jnp.sum(up * d, axis=1, keepdims=True)
    inv = 1.0 / jnp.sqrt(square / DOUT + EPS)
    slope = inner * inv
    row = lax.broadcasted_iota(jnp.int32, (16, 256), 0)
    for t in range(NT):
        cols = slice(t % half * 256, (t % half + 1) * 256)
        raw = cot_ref[t, :64, :].astype(F32)
        gain = gain_of(t)
        normed = pre[t] * inv
        grad = ((gain * raw - normed * (slope / DOUT)) * inv).astype(BF16)
        if t < half:
            pga_ref[:, cols] = grad
        else:
            pgb_ref[:, cols] = grad
        total = jnp.sum(raw * normed, axis=0, keepdims=True)
        hi = total.astype(BF16).astype(F32)
        extra = jnp.where(row == 0, hi, jnp.where(row == 1, total - hi, 0.0))
        gg_ref[t] = extra.astype(BF16)
        out_ref[t] = (gain * normed).astype(BF16)


def norm(ka, ra, kb, rb, cot):
    whole = pl.BlockSpec(memory_space=pltpu.VMEM)
    return pl.pallas_call(
        norm_kernel,
        in_specs=[whole] * 7,
        out_specs=[whole] * 4,
        out_shape=[
            jax.ShapeDtypeStruct((NT, 64, 256), BF16),
            jax.ShapeDtypeStruct((64, HALF), BF16),
            jax.ShapeDtypeStruct((64, HALF), BF16),
            jax.ShapeDtypeStruct((NT, 16, 256), BF16),
        ],
        scratch_shapes=[pltpu.VMEM((NT, 64, 256), F32)],
        compiler_params=params(),
        cost_estimate=cost(0, 6 << 20),
        name="norm",
    )(ka, ra, kb, *rb, cot)


def grad_kernel(ng, *refs):
    out = refs[-1]
    g = jnp.concatenate([g[...] for g in refs[:ng]], axis=0)
    both = tn(g, refs[ng][...])
    for s in range(3):
        out[s] = both[:, s * 256 : (s + 1) * 256]


def grad(which, gs, x, into=None):
    tile = 512
    steps = HALF // tile
    base = which * steps
    specs = [pl.BlockSpec((g.shape[0], tile), lambda j: (0, j)) for g in gs]
    specs.append(pl.BlockSpec(x.shape, lambda j: (0, 0)))
    args = list(gs) + [x]
    if into is not None:
        specs.append(pl.BlockSpec(memory_space=pl.ANY))
        args.append(into)
    return pl.pallas_call(
        functools.partial(grad_kernel, len(gs)),
        grid=(steps,),
        in_specs=specs,
        out_specs=pl.BlockSpec((3, tile, 256), lambda j: (0, base + j, 0)),
        out_shape=jax.ShapeDtypeStruct((3, DOUT, 256), F32),
        input_output_aliases={} if into is None else {len(args) - 1: 0},
        compiler_params=params(BIG),
        cost_estimate=cost(1024 * 768 * HALF, 12 << 20),
        name="grad",
    )(*args)


def local(
    attn_out,
    o_proj,
    high_resid,
    low_hidden,
    mid_hidden,
    route_list,
    fc_weight,
    norm_gain,
    cotangent,
):
    trainers = lax.axis_size("dp")
    toks = route_list.shape[0]
    cap = toks // 2
    slots = trainers * cap
    t = lax.axis_index("tensor")
    x, z, c = t // 4, t // 2 % 2, t % 2
    pos = jnp.stack([x, z, c]).astype(jnp.int32)

    here = jnp.arange(toks, dtype=jnp.int32)
    same = (route_list[:, None] == route_list[None, :]) & (here[None, :] < here[:, None])
    within = jnp.sum(same.astype(jnp.int32), axis=1)

    def onehot(slot, n):
        return (slot[:, None] == jnp.arange(n, dtype=jnp.int32)[None, :]).astype(BF16)

    pick = onehot(route_list * cap + within, slots)
    back_pick = onehot(within // 8 * 80 + route_list * 8 + within % 8, NT * 80)

    def moved(order, v):
        return jnp.dot(order, v, preferred_element_type=BF16)

    def packed(pick, v):
        return lax.dot_general(pick, v, (((0,), (1,)), ((), ())), preferred_element_type=BF16)

    early = packed(pick, jnp.concatenate([low_hidden, mid_hidden, cotangent], axis=0))
    early = lax.all_to_all(early.reshape(trainers, cap, -1), "dp", 0, 0).reshape(slots, -1)

    own, oth = oproj_partial(pos, o_proj, attn_out)
    own = own + send(oth, dc=1)
    w = jnp.transpose(fc_weight[0], (1, 0, 2))
    w, own = lax.optimization_barrier((w, own))
    w_other = send(w, dc=1)
    narrow = own.astype(BF16)
    sums = own[0]
    for dx in range(1, NX):
        sums = sums + send(narrow[dx], dx).astype(F32)
    at = jnp.arange(slots, dtype=jnp.int32)
    at, sums = lax.optimization_barrier((at, sums))
    inner = at // 8 % 8 * cap + at % 8
    block = at // 64

    def device(dc, dx, dz):
        return (x + dx) % 4 * 4 + (z ^ dz) * 2 + (c ^ dc)

    straight = onehot(inner + block * 8, slots)
    from_a = device(block // 8, block // 2 % 4, block % 2) * 8
    order_a = onehot(inner + from_a, slots)
    y, zl = lax.axis_index("dp") // 2, lax.axis_index("dp") % 2
    replica = at // 8 % 8
    apart = (y - replica // 2 + 4) % 4 * 2 + (replica % 2 ^ zl)
    near_order = onehot(apart * cap + at % 8 + from_a, slots)
    towards = (route_list % 2 ^ zl) * 4 + (route_list // 2 - y + 4) % 4
    near_pick = onehot(towards * cap + within, slots)
    order_b = onehot((block // 8 * 8 + block % 4 * 2 + block // 4 % 2) * 64 + at % 64, slots)

    term = sums[0] + send(sums[1].astype(BF16), dz=1).astype(F32)
    high_hidden = (high_resid.astype(F32) + term).astype(BF16)

    early, high_hidden = lax.optimization_barrier((early, high_hidden))

    gain = norm_gain[0]
    part0 = lax.reduce_precision(gain, 8, 7)
    part1 = lax.reduce_precision(gain - part0, 8, 7)
    part2 = gain - part0 - part1
    parts = jnp.pad(jnp.stack([part0, part1, part2]).astype(BF16), ((0, 13), (0, 0)))
    cot = jnp.concatenate(
        [
            moved(straight, early[:, 512:]).reshape(NT, 64, 256),
            jnp.broadcast_to(parts[None], (NT, 16, 256)),
        ],
        axis=1,
    )
    cot = lax.all_to_all(cot, "tensor", 0, 0)

    lowmid = early[:, :512]
    keep, other = [packed(near_pick[:, i * 512 : (i + 1) * 512], high_hidden) for i in range(2)]
    got = lax.ppermute(other, "dp", [(i, i ^ 1) for i in range(8)])
    pair = jnp.stack([keep.reshape(4, cap, -1), got.reshape(4, cap, -1)], axis=1)
    far = [
        lax.ppermute(pair[dy], "dp", [(i, (i + 2 * dy) % 8) for i in range(8)])
        for dy in range(1, 4)
    ]
    high_rows = jnp.concatenate([pair[0]] + far, axis=0).reshape(slots, -1)
    xo, xs = moved(order_a[:512], lowmid), moved(order_a[512:], lowmid)
    xp = send(xs, dc=1)
    ho, hs = moved(near_order[:512], high_rows), moved(near_order[512:], high_rows)
    hp = send(hs, dc=1)
    ho, hp, cot = lax.optimization_barrier((ho, hp, cot))

    b = join(1, xo, xp, ho, hp, w, w_other)
    bz = b[0] + send(b[1], dz=1).astype(F32)
    a = join(0, xo, xp, ho, hp, w, w_other)
    a, xs, hs = lax.optimization_barrier((a, xs, hs))
    got = [send(a[dx], dx) for dx in range(1, NX)]
    got, _ = lax.optimization_barrier((got, bz))
    ax = a[0] + got[0].astype(F32) + got[1].astype(F32) + got[2].astype(F32)
    az = send(ax[64:].astype(BF16), dz=1)
    bx = [send(bz[dx * 64 : (dx + 1) * 64].astype(BF16), dx) for dx in range(1, NX)]

    xa = jnp.concatenate(
        [jnp.concatenate([xo, xs], axis=0), jnp.concatenate([ho, hs], axis=0)], axis=1
    )
    xb = moved(order_b, xa)
    xa, xb, az = lax.optimization_barrier((xa, xb, az))

    outputs, ga, gb, gg = norm(ax[:64], az, bz[:64], bx, cot)

    far = send(ga, dz=1)
    near = [send(gb, -dx) for dx in range(1, NX)]
    outputs = outputs.reshape(NT, trainers, 8, 256).transpose(1, 0, 2, 3)
    outputs = lax.all_to_all(outputs, "dp", 0, 0)
    a0 = jnp.concatenate([ga, far], axis=0)
    near, _, outputs = lax.optimization_barrier((near, a0, outputs))
    b0 = jnp.concatenate([gb] + near, axis=0)
    a1 = [send(a0, -dx) for dx in range(1, NX)]
    b1 = send(b0, dz=1)
    a0p, b0p = send(a0, dc=1), send(b0, dc=1)
    outputs = outputs.transpose(1, 0, 2, 3).reshape(NT, 64, 256)
    outputs = jnp.concatenate([outputs, gg], axis=1)
    a1[0], outputs = lax.optimization_barrier((a1[0], outputs))
    a1p, b1p = [send(v, dc=1) for v in a1], send(b1, dc=1)
    returned = lax.all_to_all(outputs, "tensor", 0, 0)
    fc = grad(0, [a0] + a1 + [a0p] + a1p, xa)
    fc = grad(1, (b0, b1, b0p, b1p), xb, fc)
    returned, fc = lax.optimization_barrier((returned, fc))
    gain_grad = jnp.sum(returned[:, 64:66].astype(F32), axis=(0, 1))[None, :]
    draft_hidden = lax.dot_general(
        returned.reshape(NT * 80, 256),
        back_pick,
        (((0,), (1,)), ((), ())),
        preferred_element_type=BF16,
    )
    fc_grad = jnp.transpose(fc, (1, 0, 2))[None]
    return (draft_hidden, fc_grad, gain_grad)


def solution(mesh):
    return jax.shard_map(
        local,
        mesh=mesh,
        in_specs=(
            P("tensor", "dp"),
            P(None, "tensor"),
            P("tensor", "dp"),
            P("tensor", "dp"),
            P("tensor", "dp"),
            P("dp"),
            P("dp", None, None, "tensor"),
            P("dp", "tensor"),
            P("tensor", "dp"),
        ),
        out_specs=(P("tensor", "dp"), P("dp", None, None, "tensor"), P("dp", "tensor")),
        check_vma=False,
    )
```
